32 devices in a mesh: band: 4 (over x, core), blk: 8 (over z, y).
Axes of the slice: x: 2, y: 2, z: 4, core: 2. Of those that a mesh axis runs over, the one named last changes fastest.
Arguments:
- alm: bfloat16 [1024, 12, 16, 2, 1024], P('blk', None, 'band'), may hold values from -6 to 6
- legendre: bfloat16 [1024, 1024, 128], P('blk'), may hold values from -0.005859375 to 0.005859375
- orders: int32 [1024], replicated, may hold values from 0 to 1023, as said below
- data_map: bfloat16 [16, 256, 2048], P('band', 'blk'), may hold values from -8 to 8
- noise_inv: float32 [16, 256, 2048], P('band', 'blk'), may hold values from 0.1 to 1
- mixing: bfloat16 [5, 16, 256, 2048], P(None, 'band', 'blk'), may hold values from -1.5 to 1.5
Outputs:
- components: float32 [12, 5, 256, 2048], P(None, None, ('blk', 'band'))
The draws below stay inside these ranges and needn't reach their ends.
Inputs may be any that keep to these rules, and one draw needn't show every extreme that they name: Slots 2i and 2i + 1 hold a pair of orders m and 1023 - m; every order from 0 to 1023 stands in exactly one slot.
All inputs are finite; a program needn't handle non-finite values.
Results may differ from the reference program's by a relative error of at most 0.005.
Values may be sent and summed in bfloat16 or wider, within the bound.
No kernel may reach another device: no remote copies, remote signals or barrier semaphores. Data moves between devices by JAX's collectives and lax.ppermute only.
A program may use at most 192 MiB of HBM per device.

```python
import math
import jax
import jax.numpy as jnp
from jax import lax

L = 1024
M = 1024
NPHI = 2048
BANDS = 16
COMP = 5
CHAINS = 12
CIRCLES = 256


def draw_orders(key, part):
    pairs = jax.random.permutation(key, M // 2).astype(jnp.int32)
    slot_index = jnp.arange(M, dtype=jnp.int32)
    first_order = pairs[slot_index // 2]
    return jnp.where(slot_index % 2 == 0, first_order, M - 1 - first_order).astype(jnp.int32)


def block_levels(key, extent, split, least, high):
    def one(position, parts):
        heights = jax.random.uniform(jax.random.fold_in(jax.random.fold_in(key, 6), position), (parts,), jnp.float32, least / len(split), high / len(split))
        return jnp.repeat(jnp.exp(heights), extent[position] // parts).reshape((-1,) + (1,) * (len(extent) - position - 1))

    factor_of = one(*split[0])
    for cut in split[1:]:
        factor_of = factor_of * one(*cut)
    return factor_of


def noise(key, extent, scale, bound, split=(), kind=jnp.bfloat16):
    array = scale * jax.random.normal(key, extent, jnp.float32)
    if split:
        array = array * block_levels(key, extent, split, -0.22, 0.18)
    return jnp.clip(array, -bound, bound).astype(kind)


def setup_inputs(seed: int = 0) -> dict:
    key_list = jax.random.split(jax.random.key(seed), 7)
    return {
        "alm": noise(key_list[0], (M, CHAINS, BANDS, 2, L), 1.0, 6.0, ((0, 8), (2, 4))),
        "legendre": noise(key_list[1], (M, L, CIRCLES // 2), (L * M) ** -0.5, 0.005859375, ((0, 8),)),
        "orders": draw_orders(jax.random.fold_in(key_list[6], 71), 0),
        "data_map": noise(key_list[3], (BANDS, CIRCLES, NPHI), 2.0, 8.0, ((0, 4), (1, 8))),
        "noise_inv": jnp.clip(jnp.exp(math.log(1.0) - 2.3025851 * jax.random.uniform(key_list[4], (BANDS, CIRCLES, NPHI), jnp.float32) ** block_levels(key_list[4], (BANDS, CIRCLES, NPHI), ((0, 4), (1, 8)), -0.2, 0.2)), 0.1, 1.0),
        "mixing": noise(key_list[5], (COMP, BANDS, CIRCLES, NPHI), BANDS ** -0.5, 1.5, ((1, 4), (2, 8))),
    }


def dft_basis(orders, nphi):
    longitude = jnp.arange(nphi, dtype=jnp.int32)
    phase_index = (orders[:, None] * longitude[None, :]) % nphi
    angles = (2.0 * math.pi / nphi) * phase_index.astype(jnp.float32)
    weights = jnp.where(orders == 0, 1.0, 2.0).astype(jnp.float32)[:, None]
    return jnp.stack([weights * jnp.cos(angles), -weights * jnp.sin(angles)], axis=1).astype(jnp.bfloat16)


def reference(alm, legendre, orders, data_map, noise_inv, mixing):
    degree = jnp.arange(L, dtype=jnp.int32)
    sign_table = (1 - 2 * ((degree[None, :] + orders[:, None]) % 2)).astype(jnp.float32)

    def synthesise(operands):
        coefficients, table, sign_row = operands
        wide_coeff = coefficients.astype(jnp.float32)
        wide_table = table.astype(jnp.float32)
        north_part = jnp.einsum("cbjl,lr->cbjr", wide_coeff, wide_table)
        south_part = jnp.einsum("cbjl,lr->cbjr", wide_coeff * sign_row, wide_table)
        circle_values = jnp.concatenate([north_part, south_part[..., ::-1]], axis=-1)
        return circle_values.astype(jnp.bfloat16)

    spectra = lax.map(synthesise, (alm, legendre, sign_table))
    spectra = jnp.moveaxis(spectra, 1, 0)
    basis_table = dft_basis(orders, NPHI).astype(jnp.float32)
    wide_mixing = mixing.astype(jnp.float32)
    data_wide = data_map.astype(jnp.float32)

    def one_chain(chain_spec):
        sky_map = jnp.einsum("mbjr,mjp->brp", chain_spec.astype(jnp.float32), basis_table)
        weighted = (noise_inv * (data_wide - sky_map)).astype(jnp.bfloat16)
        return jnp.einsum("kbrp,brp->krp", wide_mixing, weighted.astype(jnp.float32))

    return lax.map(one_chain, spectra)
```

```python
import functools
import math

import jax
import jax.numpy as jnp
from jax import lax
from jax.experimental import pallas as pl
from jax.experimental.pallas import tpu as pltpu
from jax.sharding import PartitionSpec as P

LANES = 128
VMEM_BYTES = 60 * 2**20
CHUNKS = (1,)


def dft_basis(orders, nphi):
    longitude = jnp.arange(nphi, dtype=jnp.int32)
    phase_index = orders[:, None] * longitude[None, :] % nphi
    angles = 2.0 * math.pi / nphi * phase_index.astype(jnp.float32)
    weights = jnp.where(orders == 0, 1.0, 2.0).astype(jnp.float32)[:, None]
    return jnp.stack([weights * jnp.cos(angles), -weights * jnp.sin(angles)], axis=1).astype(
        jnp.bfloat16
    )


def synthesis_kernel(
    dims, orders_ref, alm_ref, legendre_ref, out_ref, alm_buf, leg_buf, values, out_buf, sems, out_sems
):
    first_chain, chains, per_step, buffers = dims
    slots, degrees, rings = legendre_ref.shape
    bands, parts = alm_ref.shape[2], alm_ref.shape[3]
    steps = slots // per_step
    rows = chains * bands * parts
    circles = 2 * rings // out_ref.shape[0]
    width = values.shape[2]
    tiles = rings // width

    def fetch(step, slot):
        where = pl.ds(step * per_step, per_step)
        return (
            pltpu.make_async_copy(
                alm_ref.at[where, pl.ds(first_chain, chains)], alm_buf.at[slot], sems.at[slot, 0]
            ),
            pltpu.make_async_copy(legendre_ref.at[where], leg_buf.at[slot], sems.at[slot, 1]),
        )

    for step in range(min(buffers - 1, steps)):
        for copy in fetch(step, step):
            copy.start()

    degree = lax.broadcasted_iota(jnp.int32, (degrees, 1), 0)
    alternate = (1 - 2 * (degree % 2)).astype(jnp.bfloat16)

    def one_step(step, carry):
        slot = lax.rem(step, buffers)
        ahead = step + buffers - 1

        @pl.when(ahead < steps)
        def _():
            for copy in fetch(ahead, lax.rem(ahead, buffers)):
                copy.start()

        for copy in fetch(step, slot):
            copy.wait()
        for t in range(per_step):
            index = step * per_step + t
            coefficients = alm_buf[slot, t].reshape(rows, degrees)
            table = leg_buf[slot, t]
            both = jnp.concatenate([table, table * alternate], axis=1)
            sums = jnp.dot(coefficients, both, preferred_element_type=jnp.float32)
            parity = (1 - 2 * (orders_ref[index] % 2)).astype(jnp.float32)
            for tile in range(2 * tiles):
                piece = sums[:, tile * width : (tile + 1) * width]
                values[tile, pl.ds(index * rows, rows), :] = piece if tile < tiles else piece * parity
        return carry

    lax.fori_loop(0, steps, one_step, 0)

    row = lax.broadcasted_iota(jnp.int32, (width, width), 0)
    column = lax.broadcasted_iota(jnp.int32, (width, width), 1)
    reverse = (row + column == width - 1).astype(jnp.bfloat16)
    owners = width // circles

    def store(chain, slot):
        return pltpu.make_async_copy(out_buf.at[slot], out_ref.at[:, chain], out_sems.at[slot])

    def one_chain(chain, carry):
        slot = lax.rem(chain, 2)

        @pl.when(chain >= 2)
        def _():
            store(chain - 2, slot).wait()

        for tile in range(2 * tiles):
            target = tile if tile < tiles else 3 * tiles - 1 - tile
            for part in range(parts):
                turned = []
                for band in range(bands):
                    first = (chain * bands + band) * parts + part
                    piece = values[tile, pl.ds(first, slots, stride=rows), :].astype(jnp.bfloat16)
                    if tile < tiles:
                        piece = piece.astype(jnp.float32).T
                    else:
                        piece = lax.dot_general(
                            reverse, piece, (((1,), (1,)), ((), ())), preferred_element_type=jnp.float32
                        )
                    turned.append(piece.reshape(owners, circles, slots))
                out_buf[slot, target * owners : (target + 1) * owners, part] = jnp.concatenate(
                    turned, axis=1
                ).astype(jnp.bfloat16)
        store(chain, slot).start()
        return carry

    lax.fori_loop(0, chains, one_chain, 0)
    for chain in range(max(chains - 2, 0), chains):
        store(chain, chain % 2).wait()


def synthesise(orders, alm, legendre, first_chain, chains, owners):
    slots, _, bands, parts, degrees = alm.shape
    rings = legendre.shape[2]
    circles = 2 * rings // owners
    per_step = max(n for n in (1, 2, 4) if slots % n == 0)
    buffers = 6
    rows = chains * bands * parts
    width = min(rings, LANES)
    out = (owners, chains, parts, bands * circles, slots)
    return pl.pallas_call(
        functools.partial(synthesis_kernel, (first_chain, chains, per_step, buffers)),
        out_shape=jax.ShapeDtypeStruct(out, jnp.bfloat16),
        in_specs=[
            pl.BlockSpec(memory_space=pltpu.SMEM),
            pl.BlockSpec(memory_space=pl.ANY),
            pl.BlockSpec(memory_space=pl.ANY),
        ],
        out_specs=pl.BlockSpec(memory_space=pl.ANY),
        scratch_shapes=[
            pltpu.VMEM((buffers, per_step, chains, bands, parts, degrees), jnp.bfloat16),
            pltpu.VMEM((buffers, per_step, degrees, rings), jnp.bfloat16),
            pltpu.VMEM((2 * rings // width, slots * rows, width), jnp.float32),
            pltpu.VMEM((2, owners, parts, bands * circles, slots), jnp.bfloat16),
            pltpu.SemaphoreType.DMA((buffers, 2)),
            pltpu.SemaphoreType.DMA((2,)),
        ],
        compiler_params=pltpu.CompilerParams(vmem_limit_bytes=VMEM_BYTES),
        cost_estimate=pl.CostEstimate(
            flops=4 * slots * rows * degrees * rings,
            bytes_accessed=2 * slots * degrees * (rows + rings) + 4 * slots * rows * rings,
            transcendentals=0,
        ),
    )(orders, alm, legendre)


def projection_kernel(
    dims, me_ref, spectra_ref, basis_ref, noise_ref, data_ref, mixing_ref, out_ref, left, sky
):
    groups, width = dims
    blocks, chains, parts, deep, lanes = spectra_ref.shape
    spreads = blocks // groups
    components, all_bands, circles, nphi = mixing_ref.shape
    me = me_ref[0]
    for chain in range(chains):
        for k in range(groups):
            source = lax.rem(me - k + groups, groups)
            at = (chain * groups + k) * deep
            for spread in range(spreads):
                for part in range(parts):
                    column = (spread * parts + part) * lanes
                    left[at : at + deep, column : column + lanes] = spectra_ref[
                        spread * groups + source, chain, part
                    ]

    def one_tile(tile, carry):
        start = pl.multiple_of(tile * width, width)
        sky[...] = jnp.dot(left[...], basis_ref[:, pl.ds(start, width)], preferred_element_type=jnp.float32)
        for inner in range(width // LANES):
            here = pl.ds(pl.multiple_of(start + inner * LANES, LANES), LANES)
            for chain in range(chains):
                totals = [None] * components
                for band in range(all_bands):
                    at = (chain * all_bands + band) * circles
                    value = sky[at : at + circles, inner * LANES : (inner + 1) * LANES]
                    weighted = noise_ref[band, :, here] * (data_ref[band, :, here] - value)
                    weighted = weighted.astype(jnp.bfloat16).astype(jnp.float32)
                    for component in range(components):
                        term = mixing_ref[component, band, :, here] * weighted
                        totals[component] = term if band == 0 else totals[component] + term
                for component in range(components):
                    out_ref[chain, component, :, here] = totals[component]
        return carry

    lax.fori_loop(0, nphi // width, one_tile, 0)


def project(me, spectra, basis, noise, data, mixing, groups):
    blocks, chains, parts, deep, lanes = spectra.shape
    components, all_bands, circles, nphi = mixing.shape
    at_once = max(n for n in (1, 2) if chains % n == 0)
    width = 512
    depth = basis.shape[0]
    whole = lambda shape: pl.BlockSpec(shape, lambda i: (0,) * len(shape), pipeline_mode=pl.Buffered(1))
    return pl.pallas_call(
        functools.partial(projection_kernel, (groups, width)),
        grid=(chains // at_once,),
        out_shape=jax.ShapeDtypeStruct((chains, components, circles, nphi), jnp.float32),
        in_specs=[
            pl.BlockSpec(memory_space=pltpu.SMEM),
            pl.BlockSpec((blocks, at_once, parts, deep, lanes), lambda i: (0, i, 0, 0, 0)),
            whole(basis.shape),
            whole(noise.shape),
            whole(data.shape),
            whole(mixing.shape),
        ],
        out_specs=pl.BlockSpec((at_once, components, circles, nphi), lambda i: (i, 0, 0, 0)),
        scratch_shapes=[
            pltpu.VMEM((at_once * all_bands * circles, depth), jnp.bfloat16),
            pltpu.VMEM((at_once * all_bands * circles, width), jnp.float32),
        ],
        compiler_params=pltpu.CompilerParams(vmem_limit_bytes=VMEM_BYTES),
        cost_estimate=pl.CostEstimate(
            flops=2 * chains * all_bands * circles * depth * nphi,
            bytes_accessed=2 * blocks * chains * parts * deep * lanes + 2 * depth * nphi,
            transcendentals=0,
        ),
    )(me, spectra, basis, noise, data, mixing)


def to_circle_owners(array, axis, groups):
    me = lax.axis_index("band")
    size = array.shape[axis] // groups
    pieces = []
    for k in range(groups):
        target = lax.rem(me + k, groups)
        piece = lax.dynamic_slice_in_dim(array, target * size, size, axis)
        if k:
            piece = lax.ppermute(piece, "band", [(i, (i + k) % groups) for i in range(groups)])
        pieces.append(piece)
    return pieces


def per_device(alm, legendre, orders, data_map, noise_inv, mixing):
    slots, chains = alm.shape[0], alm.shape[1]
    nphi = data_map.shape[2]
    groups = lax.axis_size("band")
    owners = groups * lax.axis_size("blk")
    me = lax.axis_index("band").astype(jnp.int32).reshape(1)
    local_orders = lax.dynamic_slice_in_dim(orders, lax.axis_index("blk") * slots, slots)

    maps = jnp.concatenate([mixing, data_map[None]], axis=0)
    maps = jnp.concatenate(to_circle_owners(maps, 2, groups), axis=1).astype(jnp.float32)
    mixing_here, data_here = maps[:-1], maps[-1]
    noise_here = jnp.concatenate(to_circle_owners(noise_inv, 1, groups), axis=0)

    merge = max(1, LANES // slots)
    lanes = merge * slots
    basis = dft_basis(orders, nphi).reshape(-1, lanes, 2, nphi)
    basis = jnp.swapaxes(basis, 1, 2).reshape(-1, nphi)

    bounds = [chains * sum(CHUNKS[:i]) // sum(CHUNKS) for i in range(len(CHUNKS) + 1)]
    results = []
    for low, high in zip(bounds[:-1], bounds[1:]):
        if low == high:
            continue
        outgoing = synthesise(local_orders, alm, legendre, low, high - low, owners)
        spectra = lax.all_to_all(outgoing, ("blk", "band"), 0, 0, tiled=True)
        if merge > 1:
            spectra = spectra.reshape((-1, merge, groups) + spectra.shape[1:])
            spectra = jnp.moveaxis(spectra, 1, 5)
            spectra = spectra.reshape((-1,) + spectra.shape[2:5] + (lanes,))
        results.append(project(me, spectra, basis, noise_here, data_here, mixing_here, groups))
    return results[0] if len(results) == 1 else jnp.concatenate(results, axis=0)


def solution(mesh):
    placed = (
        P("blk", None, "band", None, None),
        P("blk", None, None),
        P(),
        P("band", "blk", None),
        P("band", "blk", None),
        P(None, "band", "blk", None),
    )
    return jax.shard_map(
        per_device,
        mesh=mesh,
        in_specs=placed,
        out_specs=P(None, None, ("blk", "band"), None),
        check_vma=False,
    )
```

```python
import functools
import math

import jax
import jax.numpy as jnp
from jax import lax
from jax.experimental import pallas as pl
from jax.experimental.pallas import tpu as pltpu
from jax.sharding import PartitionSpec as P

LANES = 128
VMEM_BYTES = 24 * 2**20
WIDE_ROWS = 48
CHUNKS = (4, 8)


def dft_basis(orders, slots, nphi):
    pairs = orders.reshape(-1, slots // 2, 2)
    turned = pairs[:, :, 0] % 2 == 1
    even = jnp.where(turned, pairs[:, :, 1], pairs[:, :, 0])
    odd = jnp.where(turned, pairs[:, :, 0], pairs[:, :, 1])
    orders = jnp.stack([even, odd])[..., None]
    longitude = jnp.arange(nphi // 2, dtype=jnp.int32)
    phase_index = orders * longitude % nphi
    angles = 2.0 * math.pi / nphi * phase_index.astype(jnp.float32)
    weights = jnp.where(orders == 0, 1.0, 2.0).astype(jnp.float32)
    table = jnp.stack([weights * jnp.cos(angles), -weights * jnp.sin(angles)], axis=2)
    return table.astype(jnp.bfloat16).reshape(2, -1, nphi // 2)


def synthesis_kernel(
    dims, orders_ref, alm_ref, legendre_ref, out_ref, alm_buf, leg_buf, values, out_buf, sems, out_sems
):
    first_chain, chains, per_step, buffers, wide = dims
    slots, degrees, rings = legendre_ref.shape
    bands, parts = alm_ref.shape[2], alm_ref.shape[3]
    steps = slots // per_step
    rows = chains * bands * parts
    circles = 2 * rings // out_ref.shape[0]
    width = values.shape[2]
    tiles = rings // width

    def fetch(step, slot):
        where = pl.ds(step * per_step, per_step)
        return (
            pltpu.make_async_copy(
                alm_ref.at[where, pl.ds(first_chain, chains)], alm_buf.at[slot], sems.at[slot, 0]
            ),
            pltpu.make_async_copy(legendre_ref.at[where], leg_buf.at[slot], sems.at[slot, 1]),
        )

    for step in range(min(buffers - 1, steps)):
        for copy in fetch(step, step):
            copy.start()

    shape = (degrees, 1) if wide else (1, degrees)
    degree = lax.broadcasted_iota(jnp.int32, shape, 0 if wide else 1)
    alternate = (1 - 2 * (degree % 2)).astype(jnp.bfloat16)

    def one_step(step, carry):
        slot = lax.rem(step, buffers)
        ahead = step + buffers - 1

        @pl.when(ahead < steps)
        def _():
            for copy in fetch(ahead, lax.rem(ahead, buffers)):
                copy.start()

        for copy in fetch(step, slot):
            copy.wait()
        for t in range(per_step):
            index = step * per_step + t
            coefficients = alm_buf[slot, t].reshape(rows, degrees)
            table = leg_buf[slot, t]
            odd = orders_ref[index] % 2
            place = pl.multiple_of((odd * (slots // 2) + index // 2) * rows, rows)
            parity = (1 - 2 * odd).astype(jnp.float32)
            if wide:
                both = jnp.concatenate([table, table * alternate], axis=1)
                sums = jnp.dot(coefficients, both, preferred_element_type=jnp.float32)
                halves = sums[:, :rings], sums[:, rings:] * parity
            else:
                both = jnp.concatenate([coefficients, coefficients * alternate], axis=0)
                sums = jnp.dot(both, table, preferred_element_type=jnp.float32)
                halves = sums[:rows], sums[rows:] * parity
            for tile in range(2 * tiles):
                column = tile % tiles * width
                values[tile, pl.ds(place, rows), :] = halves[tile // tiles][:, column : column + width]
        return carry

    lax.fori_loop(0, steps, one_step, 0)

    row = lax.broadcasted_iota(jnp.int32, (width, width), 0)
    column = lax.broadcasted_iota(jnp.int32, (width, width), 1)
    reverse = (row + column == width - 1).astype(jnp.bfloat16)
    owners = width // circles

    def store(chain, slot):
        return pltpu.make_async_copy(out_buf.at[slot], out_ref.at[:, chain], out_sems.at[slot])

    def one_chain(chain, carry):
        slot = lax.rem(chain, 2)

        @pl.when(chain >= 2)
        def _():
            store(chain - 2, slot).wait()

        for tile in range(2 * tiles):
            target = tile if tile < tiles else 3 * tiles - 1 - tile
            for odd in range(2):
                turned = []
                for band in range(bands):
                    piece = []
                    for part in range(parts):
                        first = odd * (slots // 2) * rows + (chain * bands + band) * parts + part
                        piece.append(values[tile, pl.ds(first, slots // 2, stride=rows), :])
                    piece = jnp.concatenate(piece, axis=0).astype(jnp.bfloat16)
                    if tile < tiles:
                        piece = piece.astype(jnp.float32).T
                    else:
                        piece = lax.dot_general(
                            reverse, piece, (((1,), (1,)), ((), ())), preferred_element_type=jnp.float32
                        )
                    turned.append(piece.reshape(owners, circles, slots))
                out_buf[slot, target * owners : (target + 1) * owners, odd] = jnp.concatenate(
                    turned, axis=1
                ).astype(jnp.bfloat16)
        store(chain, slot).start()
        return carry

    lax.fori_loop(0, chains, one_chain, 0)
    for chain in range(max(chains - 2, 0), chains):
        store(chain, chain % 2).wait()


def synthesise(orders, alm, legendre, first_chain, chains, owners):
    slots, _, bands, parts, degrees = alm.shape
    rings = legendre.shape[2]
    circles = 2 * rings // owners
    per_step = max(n for n in (1, 2, 4) if slots % n == 0)
    buffers = 6
    rows = chains * bands * parts
    wide = rows > WIDE_ROWS
    width = min(rings, LANES)
    out = (owners, chains, parts, bands * circles, slots)
    return pl.pallas_call(
        functools.partial(synthesis_kernel, (first_chain, chains, per_step, buffers, wide)),
        out_shape=jax.ShapeDtypeStruct(out, jnp.bfloat16),
        in_specs=[
            pl.BlockSpec(memory_space=pltpu.SMEM),
            pl.BlockSpec(memory_space=pltpu.HBM),
            pl.BlockSpec(memory_space=pltpu.HBM),
        ],
        out_specs=pl.BlockSpec(memory_space=pltpu.HBM),
        scratch_shapes=[
            pltpu.VMEM((buffers, per_step, chains, bands, parts, degrees), jnp.bfloat16),
            pltpu.VMEM((buffers, per_step, degrees, rings), jnp.bfloat16),
            pltpu.VMEM((2 * rings // width, slots * rows, width), jnp.float32),
            pltpu.VMEM((2, owners, parts, bands * circles, slots), jnp.bfloat16),
            pltpu.SemaphoreType.DMA((buffers, 2)),
            pltpu.SemaphoreType.DMA((2,)),
        ],
        compiler_params=pltpu.CompilerParams(vmem_limit_bytes=60 * 2**20),
        cost_estimate=pl.CostEstimate(
            flops=4 * slots * rows * degrees * rings,
            bytes_accessed=2 * slots * degrees * (rows + rings) + 4 * slots * rows * rings,
            transcendentals=0,
        ),
    )(orders, alm, legendre)


def projection_kernel(dims, me_ref, spectra_ref, basis_ref, *refs):
    first_chain, groups, at_once = dims
    fields, (out_ref, left, *skies, out_buf, sems, left_sems) = refs[: 2 * groups], refs[-7:]
    blocks, chains, parities, deep, lanes = spectra_ref.shape
    components, circles = out_ref.shape[1], out_ref.shape[2]
    width = basis_ref.shape[2]
    spreads = blocks // groups
    rows = groups * deep
    step, steps = pl.program_id(0), pl.num_programs(0)
    slot = lax.rem(step, 2)

    def gathered(group):
        whole = left.at[:, pl.ds(group * at_once, at_once)]
        return pltpu.make_async_copy(whole, whole, left_sems.at[group])

    @pl.when(step == 0)
    def _():
        me = me_ref[0]
        for group in range(chains // at_once):
            some = pl.ds(group * at_once, at_once)
            for k in range(groups):
                source = lax.rem(me - k + groups, groups)
                for parity in range(parities):
                    for spread in range(spreads):
                        pltpu.make_async_copy(
                            spectra_ref.at[spread * groups + source, some, parity],
                            left.at[parity, some, k, :, pl.ds(spread * lanes, lanes)],
                            left_sems.at[group],
                        ).start()

    def store(step, half):
        slot = lax.rem(step, 2)
        where = pl.ds(pl.multiple_of((half * steps + step) * width, width), width)
        return pltpu.make_async_copy(
            out_buf.at[slot, half],
            out_ref.at[pl.ds(first_chain, chains), :, :, where],
            sems.at[slot, half],
        )

    @pl.when(step >= 2)
    def _():
        for half in range(2):
            store(step - 2, half).wait()

    here_rows = at_once * rows

    def transform(group, sky):
        @pl.when(step == 0)
        def _():
            gathered(group).wait()

        for parity in range(parities):
            sky[parity] = jnp.dot(
                left[parity, group * at_once : (group + 1) * at_once].reshape(here_rows, -1),
                basis_ref[parity],
                preferred_element_type=jnp.float32,
            )

    def weigh(group, sky, column, half):
        here = slice(column, column + LANES)
        totals = {}
        for k in range(groups):
            field_ref = fields[2 * k + half]
            for row in range(0, deep, 2 * circles):
                field = [
                    field_ref[i, row : row + 2 * circles, here].astype(jnp.float32)
                    for i in range(components + 1)
                ]
                for chain in range(at_once):
                    at = slice(chain * rows + k * deep + row, chain * rows + k * deep + row + 2 * circles)
                    even, odd = sky[0, at, here], sky[1, at, here]
                    rest = field[components] - (even + odd if half == 0 else even - odd)
                    for i in range(components):
                        term = field[i] * rest
                        term = term[:circles] + term[circles:]
                        totals[chain, i] = totals[chain, i] + term if (chain, i) in totals else term
        for (chain, i), total in totals.items():
            out_buf[slot, half, group * at_once + chain, i, :, here] = total

    transform(0, skies[0])
    for group in range(chains // at_once):
        if group + 1 < chains // at_once:
            transform(group + 1, skies[(group + 1) % 2])
        for column in range(0, width, LANES):
            for half in range(2):
                weigh(group, skies[group % 2], column, half)
    for half in range(2):
        store(step, half).start()

    @pl.when(step == steps - 1)
    def _():
        for half in range(2):
            for last in range(2):
                @pl.when(step >= last)
                def _(half=half, last=last):
                    store(step - last, half).wait()


def project(me, spectra, basis, fields, result, first_chain, shape):
    blocks, chains, parities, deep, lanes = spectra.shape
    groups, depth, half = len(fields), basis.shape[1], basis.shape[2]
    count = fields[0].shape[0]
    width = min(half, 256)
    steps = half // width
    at_once = max(n for n in (1, 2, 3, 4) if chains % n == 0)
    spectra = pltpu.with_memory_space_constraint(spectra, pltpu.HBM)
    basis = pltpu.with_memory_space_constraint(basis, pltpu.HBM)
    operands, specs, aliases = [me, spectra, basis], [], {}
    specs = [
        pl.BlockSpec(memory_space=pltpu.SMEM),
        pl.BlockSpec(memory_space=pltpu.HBM),
        pl.BlockSpec((parities, depth, width), lambda i: (0, 0, i)),
    ]
    for field in fields:
        operands += [field, field]
        specs += [
            pl.BlockSpec((count, deep, width), lambda i: (0, 0, i)),
            pl.BlockSpec((count, deep, width), lambda i: (0, 0, i + steps)),
        ]
    if result is not None:
        aliases = {len(operands): 0}
        operands.append(result)
        specs.append(pl.BlockSpec(memory_space=pl.ANY))
    return pl.pallas_call(
        functools.partial(projection_kernel, (first_chain, groups, at_once)),
        grid=(steps,),
        out_shape=jax.ShapeDtypeStruct(shape, jnp.float32),
        in_specs=specs,
        out_specs=pl.BlockSpec(memory_space=pltpu.HBM),
        scratch_shapes=[
            pltpu.VMEM((parities, chains, groups, deep, depth), jnp.bfloat16),
            pltpu.VMEM((parities, at_once * groups * deep, width), jnp.float32),
            pltpu.VMEM((parities, at_once * groups * deep, width), jnp.float32),
            pltpu.VMEM((2, 2, chains) + shape[1:3] + (width,), jnp.float32),
            pltpu.SemaphoreType.DMA((2, 2)),
            pltpu.SemaphoreType.DMA((chains // at_once,)),
        ],
        input_output_aliases=aliases,
        compiler_params=pltpu.CompilerParams(vmem_limit_bytes=VMEM_BYTES),
        cost_estimate=pl.CostEstimate(
            flops=2 * parities * chains * groups * deep * depth * half,
            bytes_accessed=2 * spectra.size + 2 * basis.size + 2 * sum(f.size for f in fields),
            transcendentals=0,
        ),
    )(*operands)


def circle_fields(mixing, data_map, noise_inv, groups):
    weights = mixing.astype(jnp.float32) * noise_inv
    whole = jnp.concatenate([weights.astype(jnp.bfloat16), data_map[None]])
    me = lax.axis_index("band")
    count, bands, circles, nphi = whole.shape
    size = circles // groups
    return [
        lax.dynamic_slice_in_dim(whole, lax.rem(me + k, groups) * size, size, 2).reshape(
            count, bands * size, nphi
        )
        for k in range(groups)
    ]


def per_device(alm, legendre, orders, data_map, noise_inv, mixing):
    slots, chains = alm.shape[0], alm.shape[1]
    circles, nphi = data_map.shape[1:]
    components = mixing.shape[0]
    groups = lax.axis_size("band")
    owners = groups * lax.axis_size("blk")
    me = lax.axis_index("band").astype(jnp.int32).reshape(1)
    local_orders = lax.dynamic_slice_in_dim(orders, lax.axis_index("blk") * slots, slots)
    merge = max(1, LANES // slots)

    def exchange(outgoing):
        spectra = lax.all_to_all(outgoing, ("blk", "band"), 0, 0, tiled=True)
        if merge == 1:
            return spectra
        spectra = spectra.reshape((-1, merge, groups) + spectra.shape[1:])
        spectra = jnp.moveaxis(spectra, 1, 5)
        return spectra.reshape((-1,) + spectra.shape[2:5] + (merge * slots,))

    bounds = [chains * sum(CHUNKS[:i]) // sum(CHUNKS) for i in range(len(CHUNKS) + 1)]
    chunks = [(low, high - low) for low, high in zip(bounds[:-1], bounds[1:]) if low < high]
    arrived, fields = [], None
    for low, count in chunks:
        outgoing = synthesise(local_orders, alm, legendre, low, count, owners)
        arrived.append(exchange(outgoing))
        if fields is None:
            mixing, data_map, noise_inv, outgoing = lax.optimization_barrier(
                (mixing, data_map, noise_inv, outgoing)
            )
            fields = circle_fields(mixing, data_map, noise_inv, groups)
            fields, local_orders = lax.optimization_barrier((fields, local_orders))
            fields = [
                lax.ppermute(f, "band", [(i, (i + k) % groups) for i in range(groups)]) if k else f
                for k, f in enumerate(fields)
            ]
    orders, _ = lax.optimization_barrier((orders, outgoing))
    basis = dft_basis(orders, slots, nphi)
    result = None
    shape = (chains, components, circles // groups, nphi)
    for (low, _), spectra in zip(chunks, arrived):
        result = project(me, spectra, basis, fields, result, low, shape)
    return result


def solution(mesh):
    placed = (
        P("blk", None, "band", None, None),
        P("blk", None, None),
        P(),
        P("band", "blk", None),
        P("band", "blk", None),
        P(None, "band", "blk", None),
    )
    return jax.shard_map(
        per_device,
        mesh=mesh,
        in_specs=placed,
        out_specs=P(None, None, ("blk", "band"), None),
        check_vma=False,
    )
```

```python
import functools
import math

import jax
import jax.numpy as jnp
from jax import lax
from jax.experimental import pallas as pl
from jax.experimental.pallas import tpu as pltpu
from jax.sharding import PartitionSpec as P

LANES = 128
VMEM_BYTES = 24 * 2**20
WIDE_ROWS = 48
CHUNKS = (4, 8)


def dft_basis(orders, slots, nphi):
    pairs = orders.reshape(-1, slots // 2, 2)
    turned = pairs[:, :, 0] % 2 == 1
    even = jnp.where(turned, pairs[:, :, 1], pairs[:, :, 0])
    odd = jnp.where(turned, pairs[:, :, 0], pairs[:, :, 1])
    orders = jnp.stack([even, odd])[..., None]
    longitude = jnp.arange(nphi // 2, dtype=jnp.int32)
    phase_index = orders * longitude % nphi
    angles = 2.0 * math.pi / nphi * phase_index.astype(jnp.float32)
    weights = jnp.where(orders == 0, 1.0, 2.0).astype(jnp.float32)
    table = jnp.stack([weights * jnp.cos(angles), -weights * jnp.sin(angles)], axis=2)
    return table.astype(jnp.bfloat16).reshape(2, -1, nphi // 2)


def synthesis_kernel(
    dims, place_ref, orders_ref, alm_ref, legendre_ref, out_ref, alm_buf, leg_buf, values, out_buf, sems, out_sems
):
    first_chain, chains, per_step, buffers, wide = dims
    first_slot = place_ref[0] * legendre_ref.shape[0]
    slots, degrees, rings = legendre_ref.shape
    bands, parts = alm_ref.shape[2], alm_ref.shape[3]
    steps = slots // per_step
    rows = chains * bands * parts
    circles = 2 * rings // out_buf.shape[1]
    width = values.shape[2]
    tiles = rings // width

    def fetch(step, slot):
        where = pl.ds(step * per_step, per_step)
        return (
            pltpu.make_async_copy(
                alm_ref.at[where, pl.ds(first_chain, chains)], alm_buf.at[slot], sems.at[slot, 0]
            ),
            pltpu.make_async_copy(legendre_ref.at[where], leg_buf.at[slot], sems.at[slot, 1]),
        )

    for step in range(min(buffers - 1, steps)):
        for copy in fetch(step, step):
            copy.start()

    shape = (degrees, 1) if wide else (1, degrees)
    degree = lax.broadcasted_iota(jnp.int32, shape, 0 if wide else 1)
    alternate = (1 - 2 * (degree % 2)).astype(jnp.bfloat16)

    def one_step(step, carry):
        slot = lax.rem(step, buffers)
        ahead = step + buffers - 1

        @pl.when(ahead < steps)
        def _():
            for copy in fetch(ahead, lax.rem(ahead, buffers)):
                copy.start()

        for copy in fetch(step, slot):
            copy.wait()
        for t in range(per_step):
            index = step * per_step + t
            coefficients = alm_buf[slot, t].reshape(rows, degrees)
            table = leg_buf[slot, t]
            odd = orders_ref[first_slot + index] % 2
            place = pl.multiple_of((odd * (slots // 2) + index // 2) * rows, rows)
            parity = (1 - 2 * odd).astype(jnp.float32)
            if wide:
                both = jnp.concatenate([table, table * alternate], axis=1)
                sums = jnp.dot(coefficients, both, preferred_element_type=jnp.float32)
                halves = sums[:, :rings], sums[:, rings:] * parity
            else:
                both = jnp.concatenate([coefficients, coefficients * alternate], axis=0)
                sums = jnp.dot(both, table, preferred_element_type=jnp.float32)
                halves = sums[:rows], sums[rows:] * parity
            for tile in range(2 * tiles):
                column = tile % tiles * width
                values[tile, pl.ds(place, rows), :] = halves[tile // tiles][:, column : column + width]
        return carry

    lax.fori_loop(0, steps, one_step, 0)

    row = lax.broadcasted_iota(jnp.int32, (width, width), 0)
    column = lax.broadcasted_iota(jnp.int32, (width, width), 1)
    reverse = (row + column == width - 1).astype(jnp.bfloat16)
    owners = width // circles

    def store(chain, slot):
        return pltpu.make_async_copy(out_buf.at[slot], out_ref.at[:, chain], out_sems.at[slot])

    def one_chain(chain, carry):
        slot = lax.rem(chain, 2)

        @pl.when(chain >= 2)
        def _():
            store(chain - 2, slot).wait()

        for tile in range(2 * tiles):
            target = tile if tile < tiles else 3 * tiles - 1 - tile
            for odd in range(2):
                turned = []
                for band in range(bands):
                    piece = []
                    for part in range(parts):
                        first = odd * (slots // 2) * rows + (chain * bands + band) * parts + part
                        piece.append(values[tile, pl.ds(first, slots // 2, stride=rows), :])
                    piece = jnp.concatenate(piece, axis=0).astype(jnp.bfloat16)
                    if tile < tiles:
                        piece = piece.astype(jnp.float32).T
                    else:
                        piece = lax.dot_general(
                            reverse, piece, (((1,), (1,)), ((), ())), preferred_element_type=jnp.float32
                        )
                    turned.append(piece.reshape(owners, circles, slots))
                out_buf[slot, target * owners : (target + 1) * owners, odd] = jnp.concatenate(
                    turned, axis=1
                ).astype(jnp.bfloat16)
        store(chain, slot).start()
        return carry

    lax.fori_loop(0, chains, one_chain, 0)
    for chain in range(max(chains - 2, 0), chains):
        store(chain, chain % 2).wait()


def synthesise(place, orders, alm, legendre, first_chain, chains, owners):
    slots, _, bands, parts, degrees = alm.shape
    rings = legendre.shape[2]
    circles = 2 * rings // owners
    per_step = max(n for n in (1, 2, 4) if slots % n == 0)
    buffers = 6
    rows = chains * bands * parts
    wide = rows > WIDE_ROWS
    width = min(rings, LANES)
    out = (owners, chains, parts, bands * circles, slots)
    return pl.pallas_call(
        functools.partial(synthesis_kernel, (first_chain, chains, per_step, buffers, wide)),
        out_shape=jax.ShapeDtypeStruct(out, jnp.bfloat16),
        in_specs=[
            pl.BlockSpec(memory_space=pltpu.SMEM),
            pl.BlockSpec(memory_space=pltpu.SMEM),
            pl.BlockSpec(memory_space=pltpu.HBM),
            pl.BlockSpec(memory_space=pltpu.HBM),
        ],
        out_specs=pl.BlockSpec(memory_space=pltpu.HBM),
        scratch_shapes=[
            pltpu.VMEM((buffers, per_step, chains, bands, parts, degrees), jnp.bfloat16),
            pltpu.VMEM((buffers, per_step, degrees, rings), jnp.bfloat16),
            pltpu.VMEM((2 * rings // width, slots * rows, width), jnp.float32),
            pltpu.VMEM((2, owners, parts, bands * circles, slots), jnp.bfloat16),
            pltpu.SemaphoreType.DMA((buffers, 2)),
            pltpu.SemaphoreType.DMA((2,)),
        ],
        compiler_params=pltpu.CompilerParams(vmem_limit_bytes=63 * 2**20),
        cost_estimate=pl.CostEstimate(
            flops=4 * slots * rows * degrees * rings,
            bytes_accessed=2 * slots * degrees * (rows + rings) + 4 * slots * rows * rings,
            transcendentals=0,
        ),
    )(place, orders, alm, legendre)


def projection_kernel(dims, place_ref, spectra_ref, basis_ref, *refs):
    first_chain, groups, at_once = dims
    fields, (out_ref, left, *skies, out_buf, sems, left_sems) = refs[: 2 * groups], refs[-7:]
    spreads, _, chains, parities, deep, lanes = spectra_ref.shape
    components, circles = out_ref.shape[1], out_ref.shape[2]
    width = basis_ref.shape[2]
    step, steps = pl.program_id(0), pl.num_programs(0)
    slot = lax.rem(step, 2)

    def gathered(group):
        whole = left.at[:, :, pl.ds(group * at_once, at_once)]
        return pltpu.make_async_copy(whole, whole, left_sems.at[group])

    @pl.when(step == 0)
    def _():
        for group in range(chains // at_once):
            some = pl.ds(group * at_once, at_once)
            for k in range(groups):
                pltpu.make_async_copy(
                    spectra_ref.at[:, lax.rem(place_ref[1] - k + groups, groups), some],
                    left.at[k, :, some],
                    left_sems.at[group],
                ).start()

    def store(step, half):
        slot = lax.rem(step, 2)
        where = pl.ds(pl.multiple_of((half * steps + step) * width, width), width)
        return pltpu.make_async_copy(
            out_buf.at[slot, half],
            out_ref.at[pl.ds(first_chain, chains), :, :, where],
            sems.at[slot, half],
        )

    @pl.when(step >= 2)
    def _():
        for half in range(2):
            store(step - 2, half).wait()

    rows = groups * at_once * deep

    def transform(group, sky):
        @pl.when(step == 0)
        def _():
            gathered(group).wait()

        some = slice(group * at_once, (group + 1) * at_once)
        for parity in range(parities):
            pieces = [left[:, spread, some, parity].reshape(rows, lanes) for spread in range(spreads)]
            sky[parity] = jnp.dot(
                jnp.concatenate(pieces, axis=1), basis_ref[parity], preferred_element_type=jnp.float32
            )

    def weigh(group, sky, column, half):
        here = slice(column, column + LANES)
        totals = {}
        for k in range(groups):
            field_ref = fields[2 * k + half]
            for row in range(0, deep, 2 * circles):
                field = [
                    field_ref[i, row : row + 2 * circles, here].astype(jnp.float32)
                    for i in range(components + 1)
                ]
                for chain in range(at_once):
                    first = (k * at_once + chain) * deep + row
                    at = slice(first, first + 2 * circles)
                    even, odd = sky[0, at, here], sky[1, at, here]
                    rest = field[components] - (even + odd if half == 0 else even - odd)
                    for i in range(components):
                        term = field[i] * rest
                        term = term[:circles] + term[circles:]
                        totals[chain, i] = totals[chain, i] + term if (chain, i) in totals else term
        for (chain, i), total in totals.items():
            out_buf[slot, half, group * at_once + chain, i, :, here] = total

    transform(0, skies[0])
    for group in range(chains // at_once):
        if group + 1 < chains // at_once:
            transform(group + 1, skies[(group + 1) % 2])
        for column in range(0, width, LANES):
            for half in range(2):
                weigh(group, skies[group % 2], column, half)
    for half in range(2):
        store(step, half).start()

    @pl.when(step == steps - 1)
    def _():
        for half in range(2):
            for last in range(2):
                @pl.when(step >= last)
                def _(half=half, last=last):
                    store(step - last, half).wait()


def project(place, spectra, basis, fields, result, first_chain, shape):
    spectra = spectra.reshape((-1, len(fields)) + spectra.shape[1:])
    spreads, _, chains, parities, deep, lanes = spectra.shape
    groups, depth, half = len(fields), basis.shape[1], basis.shape[2]
    count = fields[0].shape[0]
    width = min(half, 256)
    steps = half // width
    at_once = max(n for n in range(1, 9) if chains % n == 0)
    spectra = pltpu.with_memory_space_constraint(spectra, pltpu.HBM)
    basis = pltpu.with_memory_space_constraint(basis, pltpu.HBM)
    operands, specs, aliases = [place, spectra, basis], [], {}
    specs = [
        pl.BlockSpec(memory_space=pltpu.SMEM),
        pl.BlockSpec(memory_space=pltpu.HBM),
        pl.BlockSpec((parities, depth, width), lambda i: (0, 0, i)),
    ]
    for field in fields:
        operands += [field, field]
        specs += [
            pl.BlockSpec((count, deep, width), lambda i: (0, 0, i)),
            pl.BlockSpec((count, deep, width), lambda i: (0, 0, i + steps)),
        ]
    if result is not None:
        aliases = {len(operands): 0}
        operands.append(result)
        specs.append(pl.BlockSpec(memory_space=pl.ANY))
    return pl.pallas_call(
        functools.partial(projection_kernel, (first_chain, groups, at_once)),
        grid=(steps,),
        out_shape=jax.ShapeDtypeStruct(shape, jnp.float32),
        in_specs=specs,
        out_specs=pl.BlockSpec(memory_space=pltpu.HBM),
        scratch_shapes=[
            pltpu.VMEM((groups, spreads, chains, parities, deep, lanes), jnp.bfloat16),
            pltpu.VMEM((parities, at_once * groups * deep, width), jnp.float32),
            pltpu.VMEM((parities, at_once * groups * deep, width), jnp.float32),
            pltpu.VMEM((2, 2, chains) + shape[1:3] + (width,), jnp.float32),
            pltpu.SemaphoreType.DMA((2, 2)),
            pltpu.SemaphoreType.DMA((chains // at_once,)),
        ],
        input_output_aliases=aliases,
        compiler_params=pltpu.CompilerParams(vmem_limit_bytes=VMEM_BYTES),
        cost_estimate=pl.CostEstimate(
            flops=2 * parities * chains * groups * deep * depth * half,
            bytes_accessed=2 * spectra.size + 2 * basis.size + 2 * sum(f.size for f in fields),
            transcendentals=0,
        ),
    )(*operands)


def circle_fields(mixing, data_map, noise_inv, groups):
    weights = mixing.astype(jnp.float32) * noise_inv
    whole = jnp.concatenate([weights.astype(jnp.bfloat16), data_map[None]])
    me = lax.axis_index("band")
    count, bands, circles, nphi = whole.shape
    size = circles // groups
    return [
        lax.dynamic_slice_in_dim(whole, lax.rem(me + k, groups) * size, size, 2).reshape(
            count, bands * size, nphi
        )
        for k in range(groups)
    ]


def per_device(alm, legendre, orders, data_map, noise_inv, mixing):
    slots, chains = alm.shape[0], alm.shape[1]
    circles, nphi = data_map.shape[1:]
    components = mixing.shape[0]
    groups = lax.axis_size("band")
    owners = groups * lax.axis_size("blk")
    place = jnp.stack([lax.axis_index("blk"), lax.axis_index("band")]).astype(jnp.int32)
    merge = max(1, LANES // slots)

    def exchange(outgoing):
        spectra = lax.all_to_all(outgoing, ("blk", "band"), 0, 0, tiled=True)
        if merge == 1:
            return spectra
        spectra = spectra.reshape((-1, merge, groups) + spectra.shape[1:])
        spectra = jnp.moveaxis(spectra, 1, 5)
        return spectra.reshape((-1,) + spectra.shape[2:5] + (merge * slots,))

    bounds = [chains * sum(CHUNKS[:i]) // sum(CHUNKS) for i in range(len(CHUNKS) + 1)]
    chunks = [(low, high - low) for low, high in zip(bounds[:-1], bounds[1:]) if low < high]
    arrived, fields = [], None
    for low, count in chunks:
        outgoing = synthesise(place, orders, alm, legendre, low, count, owners)
        arrived.append(exchange(outgoing))
        if fields is None:
            mixing, data_map, noise_inv, _ = lax.optimization_barrier(
                (mixing, data_map, noise_inv, outgoing)
            )
            fields = circle_fields(mixing, data_map, noise_inv, groups)
            fields, place = lax.optimization_barrier((fields, place))
            fields = [
                lax.ppermute(f, "band", [(i, (i + k) % groups) for i in range(groups)]) if k else f
                for k, f in enumerate(fields)
            ]
    later_orders, _ = lax.optimization_barrier((orders, outgoing))
    basis = dft_basis(later_orders, slots, nphi)
    result = None
    shape = (chains, components, circles // groups, nphi)
    for (low, _), spectra in zip(chunks, arrived):
        result = project(place, spectra, basis, fields, result, low, shape)
    return result


def solution(mesh):
    placed = (
        P("blk", None, "band", None, None),
        P("blk", None, None),
        P(),
        P("band", "blk", None),
        P("band", "blk", None),
        P(None, "band", "blk", None),
    )
    return jax.shard_map(
        per_device,
        mesh=mesh,
        in_specs=placed,
        out_specs=P(None, None, ("blk", "band"), None),
        check_vma=False,
    )
```

```python
import functools
import math

import jax
import jax.numpy as jnp
from jax import lax
from jax.experimental import pallas as pl
from jax.experimental.pallas import tpu as pltpu
from jax.sharding import PartitionSpec as P

LANES = 128
VMEM_BYTES = 24 * 2**20
WIDE_ROWS = 48
CHUNKS = (3, 9)


def dft_basis(orders, slots, nphi):
    pairs = orders.reshape(-1, slots // 2, 2)
    turned = pairs[:, :, 0] % 2 == 1
    even = jnp.where(turned, pairs[:, :, 1], pairs[:, :, 0])
    odd = jnp.where(turned, pairs[:, :, 0], pairs[:, :, 1])
    orders = jnp.stack([even, odd])[..., None]
    longitude = jnp.arange(nphi // 2, dtype=jnp.int32)
    phase_index = orders * longitude % nphi
    angles = 2.0 * math.pi / nphi * phase_index.astype(jnp.float32)
    weights = jnp.where(orders == 0, 1.0, 2.0).astype(jnp.float32)
    table = jnp.stack([weights * jnp.cos(angles), -weights * jnp.sin(angles)], axis=2)
    return table.astype(jnp.bfloat16).reshape(2, -1, nphi // 2)


def synthesis_kernel(
    dims, place_ref, orders_ref, alm_ref, legendre_ref, out_ref, alm_buf, leg_buf, values, out_buf, sems, out_sems
):
    first_chain, chains, per_step, buffers, wide = dims
    first_slot = place_ref[0] * legendre_ref.shape[0]
    slots, degrees, rings = legendre_ref.shape
    bands, parts = alm_ref.shape[2], alm_ref.shape[3]
    steps = slots // per_step
    rows = chains * bands * parts
    circles = 2 * rings // out_buf.shape[1]
    width = values.shape[2]
    tiles = rings // width

    def fetch(step, slot):
        where = pl.ds(step * per_step, per_step)
        return (
            pltpu.make_async_copy(
                alm_ref.at[where, pl.ds(first_chain, chains)], alm_buf.at[slot], sems.at[slot, 0]
            ),
            pltpu.make_async_copy(legendre_ref.at[where], leg_buf.at[slot], sems.at[slot, 1]),
        )

    for step in range(min(buffers - 1, steps)):
        for copy in fetch(step, step):
            copy.start()

    shape = (degrees, 1) if wide else (1, degrees)
    degree = lax.broadcasted_iota(jnp.int32, shape, 0 if wide else 1)
    alternate = (1 - 2 * (degree % 2)).astype(jnp.bfloat16)

    def one_step(step, carry):
        slot = lax.rem(step, buffers)
        ahead = step + buffers - 1

        @pl.when(ahead < steps)
        def _():
            for copy in fetch(ahead, lax.rem(ahead, buffers)):
                copy.start()

        for copy in fetch(step, slot):
            copy.wait()
        for t in range(per_step):
            index = step * per_step + t
            coefficients = alm_buf[slot, t].reshape(rows, degrees)
            table = leg_buf[slot, t]
            odd = orders_ref[first_slot + index] % 2
            place = pl.multiple_of((odd * (slots // 2) + index // 2) * rows, rows)
            parity = (1 - 2 * odd).astype(jnp.float32)
            if wide:
                both = jnp.concatenate([table, table * alternate], axis=1)
                sums = jnp.dot(coefficients, both, preferred_element_type=jnp.float32)
                halves = sums[:, :rings], sums[:, rings:] * parity
            else:
                both = jnp.concatenate([coefficients, coefficients * alternate], axis=0)
                sums = jnp.dot(both, table, preferred_element_type=jnp.float32)
                halves = sums[:rows], sums[rows:] * parity
            for tile in range(2 * tiles):
                column = tile % tiles * width
                values[tile, pl.ds(place, rows), :] = halves[tile // tiles][:, column : column + width]
        return carry

    lax.fori_loop(0, steps, one_step, 0)

    row = lax.broadcasted_iota(jnp.int32, (width, width), 0)
    column = lax.broadcasted_iota(jnp.int32, (width, width), 1)
    reverse = (row + column == width - 1).astype(jnp.bfloat16)
    owners = width // circles

    def store(chain, slot):
        return pltpu.make_async_copy(out_buf.at[slot], out_ref.at[:, chain], out_sems.at[slot])

    def one_chain(chain, carry):
        slot = lax.rem(chain, 2)

        @pl.when(chain >= 2)
        def _():
            store(chain - 2, slot).wait()

        for tile in range(2 * tiles):
            target = tile if tile < tiles else 3 * tiles - 1 - tile
            for odd in range(2):
                turned = []
                for band in range(bands):
                    piece = []
                    for part in range(parts):
                        first = odd * (slots // 2) * rows + (chain * bands + band) * parts + part
                        piece.append(values[tile, pl.ds(first, slots // 2, stride=rows), :])
                    piece = jnp.concatenate(piece, axis=0).astype(jnp.bfloat16)
                    if tile < tiles:
                        piece = piece.astype(jnp.float32).T
                    else:
                        piece = lax.dot_general(
                            reverse, piece, (((1,), (1,)), ((), ())), preferred_element_type=jnp.float32
                        )
                    turned.append(piece.reshape(owners, circles, slots))
                out_buf[slot, target * owners : (target + 1) * owners, odd] = jnp.concatenate(
                    turned, axis=1
                ).astype(jnp.bfloat16)
        store(chain, slot).start()
        return carry

    lax.fori_loop(0, chains, one_chain, 0)
    for chain in range(max(chains - 2, 0), chains):
        store(chain, chain % 2).wait()


def synthesise(place, orders, alm, legendre, first_chain, chains, owners):
    slots, _, bands, parts, degrees = alm.shape
    rings = legendre.shape[2]
    circles = 2 * rings // owners
    per_step = max(n for n in (1, 2, 4) if slots % n == 0)
    buffers = 6
    rows = chains * bands * parts
    wide = rows > WIDE_ROWS
    width = min(rings, LANES)
    out = (owners, chains, parts, bands * circles, slots)
    return pl.pallas_call(
        functools.partial(synthesis_kernel, (first_chain, chains, per_step, buffers, wide)),
        out_shape=jax.ShapeDtypeStruct(out, jnp.bfloat16),
        in_specs=[
            pl.BlockSpec(memory_space=pltpu.SMEM),
            pl.BlockSpec(memory_space=pltpu.SMEM),
            pl.BlockSpec(memory_space=pltpu.HBM),
            pl.BlockSpec(memory_space=pltpu.HBM),
        ],
        out_specs=pl.BlockSpec(memory_space=pltpu.HBM),
        scratch_shapes=[
            pltpu.VMEM((buffers, per_step, chains, bands, parts, degrees), jnp.bfloat16),
            pltpu.VMEM((buffers, per_step, degrees, rings), jnp.bfloat16),
            pltpu.VMEM((2 * rings // width, slots * rows, width), jnp.float32),
            pltpu.VMEM((2, owners, parts, bands * circles, slots), jnp.bfloat16),
            pltpu.SemaphoreType.DMA((buffers, 2)),
            pltpu.SemaphoreType.DMA((2,)),
        ],
        compiler_params=pltpu.CompilerParams(vmem_limit_bytes=63 * 2**20),
        cost_estimate=pl.CostEstimate(
            flops=4 * slots * rows * degrees * rings,
            bytes_accessed=2 * slots * degrees * (rows + rings) + 4 * slots * rows * rings,
            transcendentals=0,
        ),
    )(place, orders, alm, legendre)


def projection_kernel(dims, place_ref, spectra_ref, basis_ref, *refs):
    first_chain, groups, at_once = dims
    fields, (out_ref, left, *skies, out_buf, sems, left_sems) = refs[: 2 * groups], refs[-7:]
    spreads, _, chains, parities, deep, lanes = spectra_ref.shape
    components, circles = out_ref.shape[1], out_ref.shape[2]
    width = basis_ref.shape[2]
    step, steps = pl.program_id(0), pl.num_programs(0)
    slot = lax.rem(step, 2)

    def gathered(group):
        whole = left.at[:, :, pl.ds(group * at_once, at_once)]
        return pltpu.make_async_copy(whole, whole, left_sems.at[group])

    @pl.when(step == 0)
    def _():
        for group in range(chains // at_once):
            some = pl.ds(group * at_once, at_once)
            for k in range(groups):
                pltpu.make_async_copy(
                    spectra_ref.at[:, lax.rem(place_ref[1] - k + groups, groups), some],
                    left.at[k, :, some],
                    left_sems.at[group],
                ).start()

    def store(step, half):
        slot = lax.rem(step, 2)
        where = pl.ds(pl.multiple_of((half * steps + step) * width, width), width)
        return pltpu.make_async_copy(
            out_buf.at[slot, half],
            out_ref.at[pl.ds(first_chain, chains), :, :, where],
            sems.at[slot, half],
        )

    @pl.when(step >= 2)
    def _():
        for half in range(2):
            store(step - 2, half).wait()

    rows = groups * at_once * deep

    def transform(group, sky):
        @pl.when(step == 0)
        def _():
            gathered(group).wait()

        some = slice(group * at_once, (group + 1) * at_once)
        for parity in range(parities):
            pieces = [left[:, spread, some, parity].reshape(rows, lanes) for spread in range(spreads)]
            sky[parity] = jnp.dot(
                jnp.concatenate(pieces, axis=1), basis_ref[parity], preferred_element_type=jnp.float32
            )

    def weigh(group, sky, column, half):
        here = slice(column, column + LANES)
        totals = {}
        for k in range(groups):
            field_ref = fields[2 * k + half]
            for row in range(0, deep, 2 * circles):
                field = [
                    field_ref[i, row : row + 2 * circles, here].astype(jnp.float32)
                    for i in range(components + 1)
                ]
                for chain in range(at_once):
                    first = (k * at_once + chain) * deep + row
                    at = slice(first, first + 2 * circles)
                    even, odd = sky[0, at, here], sky[1, at, here]
                    rest = field[components] - (even + odd if half == 0 else even - odd)
                    for i in range(components):
                        term = field[i] * rest
                        term = term[:circles] + term[circles:]
                        totals[chain, i] = totals[chain, i] + term if (chain, i) in totals else term
        for (chain, i), total in totals.items():
            out_buf[slot, half, group * at_once + chain, i, :, here] = total

    transform(0, skies[0])
    for group in range(chains // at_once):
        if group + 1 < chains // at_once:
            transform(group + 1, skies[(group + 1) % 2])
        for column in range(0, width, LANES):
            for half in range(2):
                weigh(group, skies[group % 2], column, half)
    for half in range(2):
        store(step, half).start()

    @pl.when(step == steps - 1)
    def _():
        for half in range(2):
            for last in range(2):
                @pl.when(step >= last)
                def _(half=half, last=last):
                    store(step - last, half).wait()


def project(place, spectra, basis, fields, result, first_chain, shape):
    spectra = spectra.reshape((-1, len(fields)) + spectra.shape[1:])
    spreads, _, chains, parities, deep, lanes = spectra.shape
    groups, depth, half = len(fields), basis.shape[1], basis.shape[2]
    count = fields[0].shape[0]
    width = min(half, 256)
    steps = half // width
    at_once = max(n for n in range(1, 10) if chains % n == 0)
    spectra = pltpu.with_memory_space_constraint(spectra, pltpu.HBM)
    basis = pltpu.with_memory_space_constraint(basis, pltpu.HBM)
    operands, specs, aliases = [place, spectra, basis], [], {}
    specs = [
        pl.BlockSpec(memory_space=pltpu.SMEM),
        pl.BlockSpec(memory_space=pltpu.HBM),
        pl.BlockSpec((parities, depth, width), lambda i: (0, 0, i)),
    ]
    for field in fields:
        operands += [field, field]
        specs += [
            pl.BlockSpec((count, deep, width), lambda i: (0, 0, i)),
            pl.BlockSpec((count, deep, width), lambda i: (0, 0, i + steps)),
        ]
    if result is not None:
        aliases = {len(operands): 0}
        operands.append(result)
        specs.append(pl.BlockSpec(memory_space=pl.ANY))
    return pl.pallas_call(
        functools.partial(projection_kernel, (first_chain, groups, at_once)),
        grid=(steps,),
        out_shape=jax.ShapeDtypeStruct(shape, jnp.float32),
        in_specs=specs,
        out_specs=pl.BlockSpec(memory_space=pltpu.HBM),
        scratch_shapes=[
            pltpu.VMEM((groups, spreads, chains, parities, deep, lanes), jnp.bfloat16),
            pltpu.VMEM((parities, at_once * groups * deep, width), jnp.float32),
            pltpu.VMEM((parities, at_once * groups * deep, width), jnp.float32),
            pltpu.VMEM((2, 2, chains) + shape[1:3] + (width,), jnp.float32),
            pltpu.SemaphoreType.DMA((2, 2)),
            pltpu.SemaphoreType.DMA((chains // at_once,)),
        ],
        input_output_aliases=aliases,
        compiler_params=pltpu.CompilerParams(vmem_limit_bytes=VMEM_BYTES),
        cost_estimate=pl.CostEstimate(
            flops=2 * parities * chains * groups * deep * depth * half,
            bytes_accessed=2 * spectra.size + 2 * basis.size + 2 * sum(f.size for f in fields),
            transcendentals=0,
        ),
    )(*operands)


def circle_fields(mixing, data_map, noise_inv, groups):
    weights = mixing.astype(jnp.float32) * noise_inv
    whole = jnp.concatenate([weights.astype(jnp.bfloat16), data_map[None]])
    me = lax.axis_index("band")
    count, bands, circles, nphi = whole.shape
    size = circles // groups
    return [
        lax.dynamic_slice_in_dim(whole, lax.rem(me + k, groups) * size, size, 2).reshape(
            count, bands * size, nphi
        )
        for k in range(groups)
    ]


def per_device(alm, legendre, orders, data_map, noise_inv, mixing):
    slots, chains = alm.shape[0], alm.shape[1]
    circles, nphi = data_map.shape[1:]
    components = mixing.shape[0]
    groups = lax.axis_size("band")
    owners = groups * lax.axis_size("blk")
    place = jnp.stack([lax.axis_index("blk"), lax.axis_index("band")]).astype(jnp.int32)
    merge = max(1, LANES // slots)

    def exchange(outgoing):
        spectra = lax.all_to_all(outgoing, ("blk", "band"), 0, 0, tiled=True)
        if merge == 1:
            return spectra
        spectra = spectra.reshape((-1, merge, groups) + spectra.shape[1:])
        spectra = jnp.moveaxis(spectra, 1, 5)
        return spectra.reshape((-1,) + spectra.shape[2:5] + (merge * slots,))

    bounds = [chains * sum(CHUNKS[:i]) // sum(CHUNKS) for i in range(len(CHUNKS) + 1)]
    chunks = [(low, high - low) for low, high in zip(bounds[:-1], bounds[1:]) if low < high]
    arrived, fields = [], None
    for low, count in chunks:
        outgoing = synthesise(place, orders, alm, legendre, low, count, owners)
        arrived.append(exchange(outgoing))
        if fields is None:
            mixing, data_map, noise_inv, _ = lax.optimization_barrier(
                (mixing, data_map, noise_inv, outgoing)
            )
            fields = circle_fields(mixing, data_map, noise_inv, groups)
            fields, place = lax.optimization_barrier((fields, place))
            fields = [
                lax.ppermute(f, "band", [(i, (i + k) % groups) for i in range(groups)]) if k else f
                for k, f in enumerate(fields)
            ]
    later_orders, _ = lax.optimization_barrier((orders, outgoing))
    basis = dft_basis(later_orders, slots, nphi)
    result = None
    shape = (chains, components, circles // groups, nphi)
    for (low, _), spectra in zip(chunks, arrived):
        result = project(place, spectra, basis, fields, result, low, shape)
    return result


def solution(mesh):
    placed = (
        P("blk", None, "band", None, None),
        P("blk", None, None),
        P(),
        P("band", "blk", None),
        P("band", "blk", None),
        P(None, "band", "blk", None),
    )
    return jax.shard_map(
        per_device,
        mesh=mesh,
        in_specs=placed,
        out_specs=P(None, None, ("blk", "band"), None),
        check_vma=False,
    )
```

```python
import functools
import math

import jax
import jax.numpy as jnp
from jax import lax
from jax.experimental import pallas as pl
from jax.experimental.pallas import tpu as pltpu
from jax.sharding import PartitionSpec as P

LANES = 128
VMEM_BYTES = 24 * 2**20
WIDE_ROWS = 48
CHUNKS = (3, 9)


def dft_basis(orders, slots, nphi):
    pairs = orders.reshape(-1, slots // 2, 2)
    turned = pairs[:, :, 0] % 2 == 1
    even = jnp.where(turned, pairs[:, :, 1], pairs[:, :, 0])
    odd = jnp.where(turned, pairs[:, :, 0], pairs[:, :, 1])
    orders = jnp.stack([even, odd])[..., None]
    longitude = jnp.arange(nphi // 2, dtype=jnp.int32)
    phase_index = orders * longitude % nphi
    angles = 2.0 * math.pi / nphi * phase_index.astype(jnp.float32)
    weights = jnp.where(orders == 0, 1.0, 2.0).astype(jnp.float32)
    table = jnp.stack([weights * jnp.cos(angles), -weights * jnp.sin(angles)], axis=2)
    return table.astype(jnp.bfloat16).reshape(2, -1, nphi // 2)


def synthesis_kernel(
    dims, place_ref, orders_ref, alm_ref, legendre_ref, out_ref, alm_buf, leg_buf, values, out_buf, sems, out_sems
):
    first_chain, chains, per_step, buffers, wide = dims
    first_slot = place_ref[0] * legendre_ref.shape[0]
    slots, degrees, rings = legendre_ref.shape
    bands, parts = alm_ref.shape[2], alm_ref.shape[3]
    steps = slots // per_step
    rows = chains * bands * parts
    circles = 2 * rings // out_buf.shape[1]
    width = values.shape[2]
    tiles = rings // width

    def fetch(step, slot):
        where = pl.ds(step * per_step, per_step)
        return (
            pltpu.make_async_copy(
                alm_ref.at[where, pl.ds(first_chain, chains)], alm_buf.at[slot], sems.at[slot, 0]
            ),
            pltpu.make_async_copy(legendre_ref.at[where], leg_buf.at[slot], sems.at[slot, 1]),
        )

    for step in range(min(buffers - 1, steps)):
        for copy in fetch(step, step):
            copy.start()

    shape = (degrees, 1) if wide else (1, degrees)
    degree = lax.broadcasted_iota(jnp.int32, shape, 0 if wide else 1)
    alternate = (1 - 2 * (degree % 2)).astype(jnp.bfloat16)

    def one_step(step, carry):
        slot = lax.rem(step, buffers)
        ahead = step + buffers - 1

        @pl.when(ahead < steps)
        def _():
            for copy in fetch(ahead, lax.rem(ahead, buffers)):
                copy.start()

        for copy in fetch(step, slot):
            copy.wait()
        for t in range(per_step):
            index = step * per_step + t
            coefficients = alm_buf[slot, t].reshape(rows, degrees)
            table = leg_buf[slot, t]
            odd = orders_ref[first_slot + index] % 2
            place = pl.multiple_of((odd * (slots // 2) + index // 2) * rows, rows)
            parity = (1 - 2 * odd).astype(jnp.float32)
            if wide:
                both = jnp.concatenate([table, table * alternate], axis=1)
                sums = jnp.dot(coefficients, both, preferred_element_type=jnp.float32)
                halves = sums[:, :rings], sums[:, rings:] * parity
            else:
                both = jnp.concatenate([coefficients, coefficients * alternate], axis=0)
                sums = jnp.dot(both, table, preferred_element_type=jnp.float32)
                halves = sums[:rows], sums[rows:] * parity
            for tile in range(2 * tiles):
                column = tile % tiles * width
                values[tile, pl.ds(place, rows), :] = halves[tile // tiles][:, column : column + width]
        return carry

    lax.fori_loop(0, steps, one_step, 0)

    row = lax.broadcasted_iota(jnp.int32, (width, width), 0)
    column = lax.broadcasted_iota(jnp.int32, (width, width), 1)
    reverse = (row + column == width - 1).astype(jnp.bfloat16)
    owners = width // circles

    def store(chain, slot):
        return pltpu.make_async_copy(out_buf.at[slot], out_ref.at[:, chain], out_sems.at[slot])

    def one_chain(chain, carry):
        slot = lax.rem(chain, 2)

        @pl.when(chain >= 2)
        def _():
            store(chain - 2, slot).wait()

        for tile in range(2 * tiles):
            target = tile if tile < tiles else 3 * tiles - 1 - tile
            for odd in range(2):
                turned = []
                for band in range(bands):
                    piece = []
                    for part in range(parts):
                        first = odd * (slots // 2) * rows + (chain * bands + band) * parts + part
                        piece.append(values[tile, pl.ds(first, slots // 2, stride=rows), :])
                    piece = jnp.concatenate(piece, axis=0).astype(jnp.bfloat16)
                    if tile < tiles:
                        piece = piece.astype(jnp.float32).T
                    else:
                        piece = lax.dot_general(
                            reverse, piece, (((1,), (1,)), ((), ())), preferred_element_type=jnp.float32
                        )
                    turned.append(piece.reshape(owners, circles, slots))
                out_buf[slot, target * owners : (target + 1) * owners, odd] = jnp.concatenate(
                    turned, axis=1
                ).astype(jnp.bfloat16)
        store(chain, slot).start()
        return carry

    lax.fori_loop(0, chains, one_chain, 0, unroll=chains % 3 == 0 and chains < 9 or 1)
    for chain in range(max(chains - 2, 0), chains):
        store(chain, chain % 2).wait()


def synthesise(place, orders, alm, legendre, first_chain, chains, owners):
    slots, _, bands, parts, degrees = alm.shape
    rings = legendre.shape[2]
    circles = 2 * rings // owners
    per_step = max(n for n in (1, 2, 4) if slots % n == 0)
    buffers = 6
    rows = chains * bands * parts
    wide = rows > WIDE_ROWS
    width = min(rings, LANES)
    out = (owners, chains, parts, bands * circles, slots)
    return pl.pallas_call(
        functools.partial(synthesis_kernel, (first_chain, chains, per_step, buffers, wide)),
        out_shape=jax.ShapeDtypeStruct(out, jnp.bfloat16),
        in_specs=[
            pl.BlockSpec(memory_space=pltpu.SMEM),
            pl.BlockSpec(memory_space=pltpu.SMEM),
            pl.BlockSpec(memory_space=pltpu.HBM),
            pl.BlockSpec(memory_space=pltpu.HBM),
        ],
        out_specs=pl.BlockSpec(memory_space=pltpu.HBM),
        scratch_shapes=[
            pltpu.VMEM((buffers, per_step, chains, bands, parts, degrees), jnp.bfloat16),
            pltpu.VMEM((buffers, per_step, degrees, rings), jnp.bfloat16),
            pltpu.VMEM((2 * rings // width, (slots + 1) * rows, width), jnp.float32),
            pltpu.VMEM((2, owners, parts, bands * circles, slots), jnp.bfloat16),
            pltpu.SemaphoreType.DMA((buffers, 2)),
            pltpu.SemaphoreType.DMA((2,)),
        ],
        compiler_params=pltpu.CompilerParams(vmem_limit_bytes=63 * 2**20),
        cost_estimate=pl.CostEstimate(
            flops=4 * slots * rows * degrees * rings,
            bytes_accessed=2 * slots * degrees * (rows + rings) + 4 * slots * rows * rings,
            transcendentals=0,
        ),
    )(place, orders, alm, legendre)


def projection_kernel(dims, place_ref, spectra_ref, basis_ref, *refs):
    first_chain, groups, at_once = dims
    fields, (out_ref, left, *skies, out_buf, sems, left_sems) = refs[: 2 * groups], refs[-7:]
    spreads, _, chains, parities, deep, lanes = spectra_ref.shape
    components, circles = out_ref.shape[1], out_ref.shape[2]
    width = basis_ref.shape[2]
    step, steps = pl.program_id(0), pl.num_programs(0)
    slot = lax.rem(step, 2)

    def gathered(group):
        whole = left.at[:, :, pl.ds(group * at_once, at_once)]
        return pltpu.make_async_copy(whole, whole, left_sems.at[group])

    @pl.when(step == 0)
    def _():
        for group in range(chains // at_once):
            some = pl.ds(group * at_once, at_once)
            for k in range(groups):
                pltpu.make_async_copy(
                    spectra_ref.at[:, lax.rem(place_ref[1] - k + groups, groups), some],
                    left.at[k, :, some],
                    left_sems.at[group],
                ).start()

    def store(step, half):
        slot = lax.rem(step, 2)
        where = pl.ds(pl.multiple_of((half * steps + step) * width, width), width)
        return pltpu.make_async_copy(
            out_buf.at[slot, half],
            out_ref.at[pl.ds(first_chain, chains), :, :, where],
            sems.at[slot, half],
        )

    @pl.when(step >= 2)
    def _():
        for half in range(2):
            store(step - 2, half).wait()

    rows = groups * at_once * deep

    def transform(group, sky):
        @pl.when(step == 0)
        def _():
            gathered(group).wait()

        some = slice(group * at_once, (group + 1) * at_once)
        for parity in range(parities):
            pieces = [left[:, spread, some, parity].reshape(rows, lanes) for spread in range(spreads)]
            sky[parity] = jnp.dot(
                jnp.concatenate(pieces, axis=1), basis_ref[parity], preferred_element_type=jnp.float32
            )

    def weigh(group, sky, column, half):
        here = slice(column, column + LANES)
        totals = {}
        for k in range(groups):
            field_ref = fields[2 * k + half]
            for row in range(0, deep, 2 * circles):
                field = [
                    field_ref[i, row : row + 2 * circles, here].astype(jnp.float32)
                    for i in range(components + 1)
                ]
                for chain in range(at_once):
                    first = (k * at_once + chain) * deep + row
                    at = slice(first, first + 2 * circles)
                    even, odd = sky[0, at, here], sky[1, at, here]
                    rest = field[components] - (even + odd if half == 0 else even - odd)
                    for i in range(components):
                        term = field[i] * rest
                        term = term[:circles] + term[circles:]
                        totals[chain, i] = totals[chain, i] + term if (chain, i) in totals else term
        for (chain, i), total in totals.items():
            out_buf[slot, half, group * at_once + chain, i, :, here] = total

    transform(0, skies[0])
    for group in range(chains // at_once):
        if group + 1 < chains // at_once:
            transform(group + 1, skies[(group + 1) % 2])
        for column in range(0, width, LANES):
            for half in range(2):
                weigh(group, skies[group % 2], column, half)
    for half in range(2):
        store(step, half).start()

    @pl.when(step == steps - 1)
    def _():
        for half in range(2):
            for last in range(2):
                @pl.when(step >= last)
                def _(half=half, last=last):
                    store(step - last, half).wait()


def project(place, spectra, basis, fields, result, first_chain, shape):
    spectra = spectra.reshape((-1, len(fields)) + spectra.shape[1:])
    spreads, _, chains, parities, deep, lanes = spectra.shape
    groups, depth, half = len(fields), basis.shape[1], basis.shape[2]
    count = fields[0].shape[0]
    width = min(half, 256)
    steps = half // width
    at_once = max(n for n in range(1, 10) if chains % n == 0)
    spectra = pltpu.with_memory_space_constraint(spectra, pltpu.HBM)
    basis = pltpu.with_memory_space_constraint(basis, pltpu.HBM)
    operands, specs, aliases = [place, spectra, basis], [], {}
    specs = [
        pl.BlockSpec(memory_space=pltpu.SMEM),
        pl.BlockSpec(memory_space=pltpu.HBM),
        pl.BlockSpec((parities, depth, width), lambda i: (0, 0, i)),
    ]
    for field in fields:
        operands += [field, field]
        specs += [
            pl.BlockSpec((count, deep, width), lambda i: (0, 0, i)),
            pl.BlockSpec((count, deep, width), lambda i: (0, 0, i + steps)),
        ]
    if result is not None:
        aliases = {len(operands): 0}
        operands.append(result)
        specs.append(pl.BlockSpec(memory_space=pl.ANY))
    return pl.pallas_call(
        functools.partial(projection_kernel, (first_chain, groups, at_once)),
        grid=(steps,),
        out_shape=jax.ShapeDtypeStruct(shape, jnp.float32),
        in_specs=specs,
        out_specs=pl.BlockSpec(memory_space=pltpu.HBM),
        scratch_shapes=[
            pltpu.VMEM((groups, spreads, chains, parities, deep, lanes), jnp.bfloat16),
            pltpu.VMEM((parities, at_once * groups * deep, width), jnp.float32),
            pltpu.VMEM((parities, at_once * groups * deep, width), jnp.float32),
            pltpu.VMEM((2, 2, chains) + shape[1:3] + (width,), jnp.float32),
            pltpu.SemaphoreType.DMA((2, 2)),
            pltpu.SemaphoreType.DMA((chains // at_once,)),
        ],
        input_output_aliases=aliases,
        compiler_params=pltpu.CompilerParams(vmem_limit_bytes=VMEM_BYTES),
        cost_estimate=pl.CostEstimate(
            flops=2 * parities * chains * groups * deep * depth * half,
            bytes_accessed=2 * spectra.size + 2 * basis.size + 2 * sum(f.size for f in fields),
            transcendentals=0,
        ),
    )(*operands)


def circle_fields(mixing, data_map, noise_inv, groups):
    weights = mixing.astype(jnp.float32) * noise_inv
    whole = jnp.concatenate([weights.astype(jnp.bfloat16), data_map[None]])
    me = lax.axis_index("band")
    count, bands, circles, nphi = whole.shape
    size = circles // groups
    return [
        lax.dynamic_slice_in_dim(whole, lax.rem(me + k, groups) * size, size, 2).reshape(
            count, bands * size, nphi
        )
        for k in range(groups)
    ]


def per_device(alm, legendre, orders, data_map, noise_inv, mixing):
    slots, chains = alm.shape[0], alm.shape[1]
    circles, nphi = data_map.shape[1:]
    components = mixing.shape[0]
    groups = lax.axis_size("band")
    owners = groups * lax.axis_size("blk")
    place = jnp.stack([lax.axis_index("blk"), lax.axis_index("band")]).astype(jnp.int32)
    merge = max(1, LANES // slots)

    def exchange(outgoing):
        spectra = lax.all_to_all(outgoing, ("blk", "band"), 0, 0, tiled=True)
        if merge == 1:
            return spectra
        spectra = spectra.reshape((-1, merge, groups) + spectra.shape[1:])
        spectra = jnp.moveaxis(spectra, 1, 5)
        return spectra.reshape((-1,) + spectra.shape[2:5] + (merge * slots,))

    bounds = [chains * sum(CHUNKS[:i]) // sum(CHUNKS) for i in range(len(CHUNKS) + 1)]
    chunks = [(low, high - low) for low, high in zip(bounds[:-1], bounds[1:]) if low < high]
    arrived, fields = [], None
    for low, count in chunks:
        outgoing = synthesise(place, orders, alm, legendre, low, count, owners)
        arrived.append(exchange(outgoing))
        if fields is None:
            mixing, data_map, noise_inv, _ = lax.optimization_barrier(
                (mixing, data_map, noise_inv, outgoing)
            )
            fields = circle_fields(mixing, data_map, noise_inv, groups)
            fields, place = lax.optimization_barrier((fields, place))
            fields = [
                lax.ppermute(f, "band", [(i, (i + k) % groups) for i in range(groups)]) if k else f
                for k, f in enumerate(fields)
            ]
    later_orders, _ = lax.optimization_barrier((orders, outgoing))
    basis = dft_basis(later_orders, slots, nphi)
    result = None
    shape = (chains, components, circles // groups, nphi)
    for (low, _), spectra in zip(chunks, arrived):
        result = project(place, spectra, basis, fields, result, low, shape)
    return result


def solution(mesh):
    placed = (
        P("blk", None, "band", None, None),
        P("blk", None, None),
        P(),
        P("band", "blk", None),
        P("band", "blk", None),
        P(None, "band", "blk", None),
    )
    return jax.shard_map(
        per_device,
        mesh=mesh,
        in_specs=placed,
        out_specs=P(None, None, ("blk", "band"), None),
        check_vma=False,
    )
```
